32 devices in a mesh: clip: 4 (over z), seq: 2 (over x), fsdp: 4 (over y, core).
Axes of the slice: x: 2, y: 2, z: 4, core: 2. Of those that a mesh axis runs over, the one named last changes fastest.
Arguments:
- tokens: bfloat16 [2, 16, 16, 128, 768], P(None, ('clip', 'fsdp'), 'seq'), may hold values from -6 to 6
- cotangent: bfloat16 [2, 16, 16, 128, 768], P(None, ('clip', 'fsdp'), 'seq'), may hold values from -6 to 6
- weights: float32 [16, 768, 768], P(('clip', 'fsdp'), 'seq'), may hold values from -0.8660254 to 0.8660254, as said below
- momentum: float32 [16, 768, 768], P(('clip', 'fsdp'), 'seq'), may hold values from -448 to 448
- vectors: float32 [17, 768], replicated, may hold values from -1.2 to 1.4
Outputs:
- mixed: bfloat16 [2, 16, 16, 128, 768], P(None, ('clip', 'fsdp'), 'seq')
- input_grad: bfloat16 [2, 16, 16, 128, 768], P(None, ('clip', 'fsdp'), 'seq')
- new_momentum: float32 [16, 768, 768], P(('clip', 'fsdp'), 'seq')
- new_weights: float32 [16, 768, 768], P(('clip', 'fsdp'), 'seq')
- new_low: bfloat16 [16, 768, 768], P(('clip', 'fsdp'), 'seq')
- vector_grads: float32 [17, 768], replicated
- new_vectors: float32 [17, 768], replicated
The draws below stay inside these ranges and needn't reach their ends.
Inputs may be any that keep to these rules, and one draw needn't show every extreme that they name: `weights`: weight blocks scaled by their fan-in.
All inputs are finite; a program needn't handle non-finite values.
Results may differ from the reference program's by a relative error of at most 0.018.
Values may be sent and summed in bfloat16 or wider, within the bound.
A program may use at most 448 MiB of HBM per device.

```python
import jax
import jax.numpy as jnp
from jax import lax

D = 768
HEADS = 12
HEAD = 64
FRAMES = 16
PATCHES = 128
MICRO = 2
NS_STEPS = 2
MATS = 16
VECS = 17
CLIPS = 16
TOTAL_TOK = 65536


def draw_weights(key, part):
    key = jax.random.fold_in(key, 11)
    matrix_index = jnp.arange(MATS)
    factors = 1.0 + 3.0 * (matrix_index == 3).astype(jnp.float32) + (matrix_index == 7).astype(jnp.float32) - 0.5 * (matrix_index >= 12).astype(jnp.float32)
    sample = jnp.clip(jax.random.normal(key, (MATS, D, D), jnp.float32), -6.0, 6.0)
    return sample * factors[:, None, None] * D ** (-0.5)


def draw_vectors(key, part):
    key = jax.random.fold_in(key, 29)
    gain_key, offset_key = jax.random.split(key)
    gain_rows = 1.0 + 0.15 * jnp.clip(jax.random.normal(gain_key, (3, D), jnp.float32), -2.5, 2.5)
    offsets = 0.3 * jnp.clip(jax.random.normal(offset_key, (VECS - 3, D), jnp.float32), -4.0, 4.0)
    return jnp.concatenate([gain_rows, offsets], 0)


def block_levels(key, dims, cuts, least, largest):
    level = 1.0
    for position, blocks in cuts:
        steps = jax.random.uniform(jax.random.fold_in(jax.random.fold_in(key, 6), position), (blocks,), jnp.float32, least / len(cuts), largest / len(cuts))
        level = level * jnp.repeat(jnp.exp(steps), dims[position] // blocks).reshape((-1,) + (1,) * (len(dims) - 1 - position))
    return level


def scatter_about(own_key, shape, spread, limit, shards=(), held_as=jnp.bfloat16):
    level = block_levels(own_key, shape, shards, -0.22, 0.18) if shards else 1.0
    array = jax.random.normal(own_key, shape, jnp.float32) * spread * level
    return jnp.minimum(jnp.maximum(array, -limit), limit).astype(held_as)


def setup_inputs(seed: int = 0) -> dict:
    streams_of = jax.random.split(jax.random.key(seed), 6)
    tokens = scatter_about(streams_of[0], (MICRO, CLIPS, FRAMES, PATCHES, D), 1.0, 6.0, ((1, 16), (2, 2)))
    cotangent = scatter_about(streams_of[1], (MICRO, CLIPS, FRAMES, PATCHES, D), 1.0, 6.0, ((1, 16), (2, 2)))
    weights = draw_weights(jax.random.fold_in(streams_of[5], 71), 0)
    momentum = scatter_about(streams_of[3], (MATS, D, D), (0.3 * TOTAL_TOK ** 0.5), 448.0, ((0, 16), (1, 2)), jnp.float32)
    vectors = draw_vectors(jax.random.fold_in(streams_of[5], 71), 0)
    return dict(tokens=tokens, cotangent=cotangent, weights=weights, momentum=momentum, vectors=vectors)


EPS_NORM = 1e-06
NS_A = 3.4445
NS_B = -4.775
NS_C = 2.0315
DECAY = 0.5
MUON_RATE = 0.5
VECTOR_RATE = 0.2
HIGHEST = lax.Precision.HIGHEST

@jax.custom_vjp
def low(v):
    return lax.optimization_barrier(v.astype(jnp.bfloat16)).astype(jnp.float32)

@jax.custom_vjp
def low_back(v):
    return v

def low_keep(v):
    return (low(v), None)

def low_pass(kept, grad):
    return (grad,)

def back_keep(v):
    return (v, None)

def back_low(kept, grad):
    return (low(grad),)
low.defvjp(low_keep, low_pass)
low_back.defvjp(back_keep, back_low)

def factor_of(matrix_index):
    return 1.0 + 3.0 * (matrix_index == 3).astype(jnp.float32) + (matrix_index == 7).astype(jnp.float32) - 0.5 * (matrix_index >= 12).astype(jnp.float32)

def layer_norm(values, gain_row, offset):
    average = lax.optimization_barrier(jnp.mean(values, -1, keepdims=True))
    centred = values - average
    return centred * lax.rsqrt(lax.optimization_barrier(jnp.mean(centred * centred, -1, keepdims=True)) + EPS_NORM) * gain_row + offset

def project(values, matrix):
    return jnp.einsum('...d,de->...e', values, matrix, precision=HIGHEST)

def attend(normed, w_query, w_key, w_value, w_out, b_query, b_value, b_out):
    head_shape = (normed.shape[0], normed.shape[1], HEADS, HEAD)
    queries = low(low_back(project(normed, w_query) + b_query)).reshape(head_shape)
    key_heads = low(low_back(project(normed, w_key))).reshape(head_shape)
    value_heads = low(low_back(project(normed, w_value) + b_value)).reshape(head_shape)
    scores = low_back(jnp.einsum('bqhe,bkhe->bhqk', queries, key_heads, precision=HIGHEST) * HEAD ** (-0.5))
    chances = low(jax.nn.softmax(scores, axis=-1))
    attended = jnp.einsum('bhqk,bkhe->bqhe', chances, value_heads, precision=HIGHEST).reshape(normed.shape)
    attended = low(low_back(attended))
    return low_back(project(attended, w_out) + b_out)

def clip_layer(w_low, vector_rows, clip_tokens):
    normed_one = low(layer_norm(clip_tokens, vector_rows[0], vector_rows[3]))
    branch_one = attend(normed_one, w_low[0], w_low[1], w_low[2], w_low[3], vector_rows[6], vector_rows[7], vector_rows[8])
    first = low(low_back(clip_tokens + branch_one))
    placed = jnp.swapaxes(first, 0, 1)
    normed_two = low(layer_norm(placed, vector_rows[1], vector_rows[4]))
    branch_two = attend(normed_two, w_low[4], w_low[5], w_low[6], w_low[7], vector_rows[9], vector_rows[10], vector_rows[11])
    second = jnp.swapaxes(low(low_back(placed + branch_two)), 0, 1)
    normed_three = low(layer_norm(second, vector_rows[2], vector_rows[5]))
    hidden = low_back(jnp.einsum('fpd,jde->fpje', normed_three, w_low[8:12], precision=HIGHEST) + vector_rows[13:17])
    active = low(jax.nn.gelu(hidden, approximate=False))
    branch_three = low_back(jnp.einsum('fpje,jed->fpd', active, w_low[12:16], precision=HIGHEST) + vector_rows[12])
    return second + branch_three

def newton_schulz(matrix):
    current = matrix / (jnp.sqrt(jnp.sum(matrix * matrix)) + 1e-07)
    for sweep_index in range(NS_STEPS):
        gram_matrix = jnp.dot(current, current.T, precision=HIGHEST)
        polynomial = NS_B * gram_matrix + NS_C * jnp.dot(gram_matrix, gram_matrix, precision=HIGHEST)
        current = NS_A * current + jnp.dot(polynomial, current, precision=HIGHEST)
    return current

def reference(tokens, cotangent, weights, momentum, vectors):
    flat_shape = (MICRO * CLIPS, FRAMES, PATCHES, D)
    inputs = tokens.astype(jnp.float32).reshape(flat_shape)

    def forward(w_master, vector_rows, values):
        w_low = low(w_master)

        def advance(carried, clip_tokens):
            return (carried, jax.checkpoint(clip_layer)(w_low, vector_rows, clip_tokens))
        carried, outputs = lax.scan(advance, jnp.zeros((), jnp.float32), values)
        return outputs
    outputs, pullback = jax.vjp(forward, weights, vectors, inputs)
    grad_w, grad_v, grad_x = pullback(cotangent.astype(jnp.float32).reshape(flat_shape))
    new_momentum = DECAY * momentum + grad_w
    orthogonal = lax.map(newton_schulz, new_momentum)
    factors = factor_of(jnp.arange(MATS))[:, None, None]
    new_weights = weights - MUON_RATE * factors * orthogonal
    new_vectors = vectors - VECTOR_RATE * TOTAL_TOK ** (-0.5) * grad_v
    return (outputs.reshape(tokens.shape).astype(jnp.bfloat16), grad_x.reshape(tokens.shape).astype(jnp.bfloat16), new_momentum, new_weights, new_weights.astype(jnp.bfloat16), grad_v, new_vectors)
```

```python
import functools
import math

import jax
import jax.numpy as jnp
from jax import lax
from jax.experimental import pallas as pl
from jax.experimental.pallas import tpu as pltpu
from jax.sharding import PartitionSpec as P

HEADS = 12
HEAD = 64
FRAMES = 16
PATCHES = 128
NS_STEPS = 2


EPS_NORM = 1e-06
NS_A = 3.4445
NS_B = -4.775
NS_C = 2.0315
DECAY = 0.5
MUON_RATE = 0.5
VECTOR_RATE = 0.2
HIGHEST = lax.Precision.HIGHEST


def factor_of(matrix_index):
    return (
        1.0
        + 3.0 * (matrix_index == 3).astype(jnp.float32)
        + (matrix_index == 7).astype(jnp.float32)
        - 0.5 * (matrix_index >= 12).astype(jnp.float32)
    )


def pattern(left_form, right_form, result_form):
    return left_form + "," + right_form + "->" + result_form


def heads_view(values):
    return values.reshape(values.shape[:-1] + (HEADS, HEAD))


def flat_view(values):
    return values.reshape(values.shape[:-2] + (HEADS * HEAD,))


def multiply(values, matrix):
    return jnp.einsum("...d,de->...e", values, matrix, preferred_element_type=jnp.float32)


def multiply_back(grads, matrix):
    return jnp.einsum("...e,de->...d", grads, matrix, preferred_element_type=jnp.float32)


def outer_sum(values, grads):
    return jnp.einsum("...d,...e->de", values, grads, preferred_element_type=jnp.float32)


def token_sum(values):
    return jnp.sum(values.reshape((-1,) + values.shape[-1:]).astype(jnp.float32), 0)


def exact_gelu(values):
    return jax.nn.gelu(values, approximate=False)


def norm_forward(values, gain_row, offset):
    average = jnp.mean(values, -1, keepdims=True)
    centred = values - average
    inverse = lax.rsqrt(jnp.mean(centred * centred, -1, keepdims=True) + EPS_NORM)
    normal = centred * inverse
    return (normal, inverse, normal * gain_row + offset)


def norm_backward(grads, normal, inverse, gain_row):
    scaled = grads * gain_row
    back = inverse * (
        scaled
        - jnp.mean(scaled, -1, keepdims=True)
        - normal * jnp.mean(scaled * normal, -1, keepdims=True)
    )
    return (back, token_sum(grads * normal), token_sum(grads))


def scores_of(queries, key_heads, forms, score_scale):
    return (
        jnp.einsum(
            pattern(forms[0], forms[1], forms[2]),
            queries,
            key_heads,
            preferred_element_type=jnp.float32,
        )
        * score_scale
    )


def attention_core(queries, key_heads, value_heads, forms, score_scale):
    scores = scores_of(queries, key_heads, forms, score_scale)
    log_total = jax.nn.logsumexp(scores, axis=-1, keepdims=True)
    chances = jnp.exp(scores - log_total).astype(jnp.bfloat16)
    attended = jnp.einsum(
        pattern(forms[2], forms[1], forms[0]),
        chances,
        value_heads,
        preferred_element_type=jnp.float32,
    )
    return (attended, log_total)


def attention_grads(queries, key_heads, value_heads, log_total, grad_attended, forms, score_scale):
    chances = jnp.exp(scores_of(queries, key_heads, forms, score_scale) - log_total)
    chances_low = chances.astype(jnp.bfloat16)
    grad_chances = jnp.einsum(
        pattern(forms[0], forms[1], forms[2]),
        grad_attended,
        value_heads,
        preferred_element_type=jnp.float32,
    )
    grad_value = jnp.einsum(
        pattern(forms[2], forms[0], forms[1]),
        chances_low,
        grad_attended,
        preferred_element_type=jnp.float32,
    )
    grad_scores = (
        chances * (grad_chances - jnp.sum(grad_chances * chances, -1, keepdims=True))
    ).astype(jnp.bfloat16)
    grad_query = (
        jnp.einsum(
            pattern(forms[2], forms[1], forms[0]),
            grad_scores,
            key_heads,
            preferred_element_type=jnp.float32,
        )
        * score_scale
    )
    grad_key = (
        jnp.einsum(
            pattern(forms[2], forms[0], forms[1]),
            grad_scores,
            queries,
            preferred_element_type=jnp.float32,
        )
        * score_scale
    )
    return (grad_query, grad_key, grad_value)


def project_three(normed_low, weight_stack, first_block, vector_rows, query_row, value_row):
    queries = (multiply(normed_low, weight_stack[first_block]) + vector_rows[query_row]).astype(
        jnp.bfloat16
    )
    key_rows = multiply(normed_low, weight_stack[first_block + 1]).astype(jnp.bfloat16)
    value_rows = (
        multiply(normed_low, weight_stack[first_block + 2]) + vector_rows[value_row]
    ).astype(jnp.bfloat16)
    return (queries, key_rows, value_rows)


def out_back(attended_low, grad_low, w_out):
    d_out = outer_sum(attended_low, grad_low)
    grad_attended = multiply_back(grad_low, w_out).astype(jnp.bfloat16)
    return (d_out, token_sum(grad_low), grad_attended)


def input_back(normed_low, grad_query, grad_key, grad_value, weight_stack, first_block):
    d_query = outer_sum(normed_low, grad_query)
    d_key = outer_sum(normed_low, grad_key)
    d_value = outer_sum(normed_low, grad_value)
    grad_normed = (
        multiply_back(grad_query, weight_stack[first_block])
        + multiply_back(grad_key, weight_stack[first_block + 1])
        + multiply_back(grad_value, weight_stack[first_block + 2])
    )
    return (d_query, d_key, d_value, token_sum(grad_query), token_sum(grad_value), grad_normed)


def layer_pass(tokens_one, cotangent_one, weight_stack, vector_rows):
    score_scale = HEAD ** (-0.5)
    spatial_forms = ("cfqhe", "cfkhe", "cfhqk")
    temporal_forms = ("cqphe", "ckphe", "cphqk")
    start = tokens_one.astype(jnp.float32)
    normal_one, inverse_one, normed = norm_forward(start, vector_rows[0], vector_rows[3])
    normed_one = normed.astype(jnp.bfloat16)
    query_one, key_one, value_one = project_three(normed_one, weight_stack, 0, vector_rows, 6, 7)
    attended, log_one = attention_core(
        heads_view(query_one),
        heads_view(key_one),
        heads_view(value_one),
        spatial_forms,
        score_scale,
    )
    attended_one = flat_view(attended).astype(jnp.bfloat16)
    first = (start + multiply(attended_one, weight_stack[3]) + vector_rows[8]).astype(jnp.bfloat16)
    placed = lax.all_to_all(first, "seq", split_axis=2, concat_axis=1, tiled=True)
    placed_float = placed.astype(jnp.float32)
    normal_two, inverse_two, normed = norm_forward(placed_float, vector_rows[1], vector_rows[4])
    normed_two = normed.astype(jnp.bfloat16)
    query_two, key_two, value_two = project_three(normed_two, weight_stack, 4, vector_rows, 9, 10)
    attended, log_two = attention_core(
        heads_view(query_two),
        heads_view(key_two),
        heads_view(value_two),
        temporal_forms,
        score_scale,
    )
    attended_two = flat_view(attended).astype(jnp.bfloat16)
    second = (placed_float + multiply(attended_two, weight_stack[7]) + vector_rows[11]).astype(
        jnp.bfloat16
    )
    framed = lax.all_to_all(second, "seq", split_axis=1, concat_axis=2, tiled=True)
    framed_float = framed.astype(jnp.float32)
    normal_three, inverse_three, normed = norm_forward(framed_float, vector_rows[2], vector_rows[5])
    normed_three = normed.astype(jnp.bfloat16)
    hidden = (
        jnp.einsum(
            "cfpd,jde->cfpje", normed_three, weight_stack[8:12], preferred_element_type=jnp.float32
        )
        + vector_rows[13:17]
    )
    activated, gelu_pull = jax.vjp(exact_gelu, hidden)
    active_low = activated.astype(jnp.bfloat16)
    output = (
        framed_float
        + jnp.einsum(
            "cfpje,jed->cfpd", active_low, weight_stack[12:16], preferred_element_type=jnp.float32
        )
        + vector_rows[12]
    ).astype(jnp.bfloat16)
    grad_float = cotangent_one.astype(jnp.float32)
    d_down = jnp.einsum(
        "cfpje,cfpd->jed", active_low, cotangent_one, preferred_element_type=jnp.float32
    )
    grad_active = jnp.einsum(
        "cfpd,jed->cfpje", cotangent_one, weight_stack[12:16], preferred_element_type=jnp.float32
    )
    grad_hidden = gelu_pull(grad_active)[0].astype(jnp.bfloat16)
    d_up = jnp.einsum(
        "cfpd,cfpje->jde", normed_three, grad_hidden, preferred_element_type=jnp.float32
    )
    d_bias_up = jnp.sum(grad_hidden.astype(jnp.float32).reshape((-1,) + grad_hidden.shape[-2:]), 0)
    grad_normed = jnp.einsum(
        "cfpje,jde->cfpd", grad_hidden, weight_stack[8:12], preferred_element_type=jnp.float32
    )
    back_three, gain_three, offset_three = norm_backward(
        grad_normed, normal_three, inverse_three, vector_rows[2]
    )
    grad_second = (grad_float + back_three).astype(jnp.bfloat16)
    grad_placed = lax.all_to_all(grad_second, "seq", split_axis=2, concat_axis=1, tiled=True)
    d_out_two, bias_out_two, grad_attended = out_back(attended_two, grad_placed, weight_stack[7])
    grad_query, grad_key, grad_value = attention_grads(
        heads_view(query_two),
        heads_view(key_two),
        heads_view(value_two),
        log_two,
        heads_view(grad_attended),
        temporal_forms,
        score_scale,
    )
    d_query_two, d_key_two, d_value_two, bias_query_two, bias_value_two, grad_normed = input_back(
        normed_two,
        flat_view(grad_query).astype(jnp.bfloat16),
        flat_view(grad_key).astype(jnp.bfloat16),
        flat_view(grad_value).astype(jnp.bfloat16),
        weight_stack,
        4,
    )
    back_two, gain_two, offset_two = norm_backward(
        grad_normed, normal_two, inverse_two, vector_rows[1]
    )
    grad_first = (grad_placed.astype(jnp.float32) + back_two).astype(jnp.bfloat16)
    grad_framed = lax.all_to_all(grad_first, "seq", split_axis=1, concat_axis=2, tiled=True)
    d_out_one, bias_out_one, grad_attended = out_back(attended_one, grad_framed, weight_stack[3])
    grad_query, grad_key, grad_value = attention_grads(
        heads_view(query_one),
        heads_view(key_one),
        heads_view(value_one),
        log_one,
        heads_view(grad_attended),
        spatial_forms,
        score_scale,
    )
    d_query_one, d_key_one, d_value_one, bias_query_one, bias_value_one, grad_normed = input_back(
        normed_one,
        flat_view(grad_query).astype(jnp.bfloat16),
        flat_view(grad_key).astype(jnp.bfloat16),
        flat_view(grad_value).astype(jnp.bfloat16),
        weight_stack,
        0,
    )
    back_one, gain_one, offset_one = norm_backward(
        grad_normed, normal_one, inverse_one, vector_rows[0]
    )
    grad_input = (grad_framed.astype(jnp.float32) + back_one).astype(jnp.bfloat16)
    weight_grads = jnp.concatenate(
        [
            jnp.stack(
                [
                    d_query_one,
                    d_key_one,
                    d_value_one,
                    d_out_one,
                    d_query_two,
                    d_key_two,
                    d_value_two,
                    d_out_two,
                ]
            ),
            d_up,
            d_down,
        ],
        0,
    )
    vector_grads = jnp.concatenate(
        [
            jnp.stack(
                [
                    gain_one,
                    gain_two,
                    gain_three,
                    offset_one,
                    offset_two,
                    offset_three,
                    bias_query_one,
                    bias_value_one,
                    bias_out_one,
                    bias_query_two,
                    bias_value_two,
                    bias_out_two,
                    token_sum(grad_float),
                ]
            ),
            d_bias_up,
        ],
        0,
    )
    return (output, grad_input, weight_grads, vector_grads)


def gather_weights(low_shard):
    row_full = lax.all_gather(low_shard, "seq", axis=1, tiled=True)
    return lax.all_gather(row_full, ("clip", "fsdp"), axis=0, tiled=True)


def reduce_grads(weight_grads):
    owner_part = lax.psum_scatter(
        weight_grads.astype(jnp.bfloat16), ("clip", "fsdp"), scatter_dimension=0, tiled=True
    )
    return lax.psum_scatter(owner_part, "seq", scatter_dimension=1, tiled=True).astype(jnp.float32)


def newton_schulz(matrix):
    current = matrix / (jnp.sqrt(jnp.sum(matrix * matrix)) + 1e-07)
    for sweep_index in range(NS_STEPS):
        gram_matrix = jnp.dot(current, current.T, precision=HIGHEST)
        polynomial = NS_B * gram_matrix + NS_C * jnp.dot(
            gram_matrix, gram_matrix, precision=HIGHEST
        )
        current = NS_A * current + jnp.dot(polynomial, current, precision=HIGHEST)
    return current


def body(tokens, cotangent, weights, momentum, vectors):
    micro_count = tokens.shape[0]
    low_shard = weights.astype(jnp.bfloat16)
    owner_grads = jnp.zeros(weights.shape, jnp.float32)
    vector_total = jnp.zeros(vectors.shape, jnp.float32)
    outputs = []
    input_grads = []
    for micro_index in range(micro_count):
        weight_stack = gather_weights(low_shard)
        output, grad_input, weight_grads, vector_grads = layer_pass(
            tokens[micro_index], cotangent[micro_index], weight_stack, vectors
        )
        outputs.append(output)
        input_grads.append(grad_input)
        vector_total = vector_total + vector_grads
        owner_grads = owner_grads + reduce_grads(weight_grads)
    vector_sum = lax.psum(vector_total, ("clip", "seq", "fsdp"))
    new_momentum = DECAY * momentum + owner_grads
    full_moment = lax.all_gather(
        new_momentum.astype(jnp.bfloat16), "seq", axis=1, tiled=True
    ).astype(new_momentum.dtype)
    whole_result = jax.vmap(newton_schulz)(full_moment)
    row_count = new_momentum.shape[1]
    orthogonal = lax.dynamic_slice_in_dim(
        whole_result, lax.axis_index("seq") * row_count, row_count, 1
    )
    local_count = weights.shape[0]
    matrix_index = lax.axis_index(("clip", "fsdp")) * local_count + jnp.arange(local_count)
    new_weights = weights - MUON_RATE * factor_of(matrix_index)[:, None, None] * orthogonal
    total_tokens = (
        micro_count * tokens.shape[1] * lax.axis_size(("clip", "fsdp")) * FRAMES * PATCHES
    )
    new_vectors = vectors - VECTOR_RATE * total_tokens ** (-0.5) * vector_sum
    return (
        jnp.stack(outputs),
        jnp.stack(input_grads),
        new_momentum,
        new_weights,
        new_weights.astype(jnp.bfloat16),
        vector_sum,
        new_vectors,
    )


BF16 = jnp.bfloat16
F32 = jnp.float32
TILE = 512
BLOCK = 128
PAIRS = HEADS // 2
LOG2E = 1.4426950408889634
VMEM_LIMIT = 60 * 1024 * 1024
MESH = pl.DeviceIdType.MESH


def dot(left, right, left_dim=1, right_dim=0):
    return lax.dot_general(
        left, right, (((left_dim,), (right_dim,)), ((), ())), preferred_element_type=F32
    )


def row_stats(values):
    average = jnp.mean(values, -1, keepdims=True)
    centred = values - average
    inverse = lax.rsqrt(jnp.mean(centred * centred, -1, keepdims=True) + EPS_NORM)
    return centred * inverse, inverse


def norm_pull(grads, normal, inverse, gain_row):
    scaled = grads * gain_row
    return inverse * (
        scaled
        - jnp.mean(scaled, -1, keepdims=True)
        - normal * jnp.mean(scaled * normal, -1, keepdims=True)
    )


def column_sum(values):
    return jnp.sum(values.astype(F32), 0, keepdims=True)


def load_rows(ref, temporal):
    values = ref[...].astype(F32)
    if not temporal:
        return values
    frames, places, width = values.shape
    values = values.reshape(frames, places // 8, 8, width)
    return values.transpose(1, 0, 2, 3).reshape(frames * places, width)


def store_rows(ref, values, temporal):
    if temporal:
        frames, places, width = ref.shape
        values = values.reshape(places // 8, frames, 8, width)
        values = values.transpose(1, 0, 2, 3).reshape(frames, places, width)
    ref[...] = values.astype(ref.dtype)


def half_masks():
    lane = lax.broadcasted_iota(jnp.int32, (1, BLOCK), 1)
    low = (lane < HEAD).astype(F32)
    return low.astype(BF16), (1.0 - low).astype(BF16)


def stacked(values, masks):
    return jnp.concatenate([values * masks[0], values * masks[1]], 0)


def place_mask():
    rows = lax.broadcasted_iota(jnp.int32, (BLOCK, BLOCK), 0)
    columns = lax.broadcasted_iota(jnp.int32, (BLOCK, BLOCK), 1)
    same = lax.rem(rows, 8) == lax.rem(columns, 8)
    return jnp.concatenate([same, same], 1)


def head_sums():
    rows = lax.broadcasted_iota(jnp.int32, (2 * BLOCK, BLOCK), 0)
    lanes = lax.broadcasted_iota(jnp.int32, (2 * BLOCK, BLOCK), 1)
    return ((rows < BLOCK) == (lanes < HEAD)).astype(F32).astype(BF16)


def lane_pairs():
    return [slice(pair * BLOCK, (pair + 1) * BLOCK) for pair in range(PAIRS)]


def powers_of(scores, mask):
    if mask is not None:
        scores = jnp.where(mask, scores, -1e30)
    parts = []
    for side in range(2):
        half = scores[:, side * BLOCK : (side + 1) * BLOCK]
        top = jnp.max(half, -1, keepdims=True)
        parts.append(jnp.exp2((half - top) * (LOG2E * HEAD ** (-0.5))).astype(BF16))
    return jnp.concatenate(parts, 1)


ERF_P = 0.3275911
ERF_A = (0.254829592, -0.284496736, 1.421413741, -1.453152027, 1.061405429)
BELL = (0.5 / math.pi) ** 0.5


def gelu_pair(values):
    bell = jnp.exp2(values * values * (-0.5 * LOG2E))
    ratio = 1.0 / (1.0 + jnp.abs(values) * (ERF_P * 0.5 ** 0.5))
    tail = 0.5 * ERF_A[4]
    for term in ERF_A[3::-1]:
        tail = tail * ratio + 0.5 * term
    tail = tail * ratio * bell
    cumulative = jnp.where(values < 0.0, tail, 1.0 - tail)
    return values * cumulative, cumulative + values * bell * BELL


def feed_kernel(
    x_ref, vec_ref, w_ref, c_ref, part_ref,
    y_ref, dx_ref, dup_ref, ddown_ref, dvec_ref, mixed_ref,
    g_all, h_ref, z_ref, du_ref, y_acc, dh_acc, y_keep, blocks, sends, gots, loads,
):
    chunk = pl.program_id(0)
    chunks = pl.num_programs(0)
    step = pl.program_id(1)
    steps = pl.num_programs(1)
    tile = lax.rem(step + jnp.where(chunk == chunks - 1, steps // 2, 0), steps)
    rows = pl.ds(pl.multiple_of(tile * TILE, TILE), TILE)
    per_tile = TILE // BLOCK
    mid = g_all.shape[0] // 2
    quarter = mid // 2
    side, depth, line, core = places()
    chunk_line = lax.rem(line + chunk // 2, 2)
    chunk_core = lax.rem(core + lax.rem(chunk, 2), 2)
    hidden_block = 2 * chunk_line + chunk_core
    width = x_ref.shape[1]
    own = [pltpu.make_async_copy(w_ref.at[2 + u, line, core], blocks.at[u, 0], loads.at[u]) for u in range(2)]
    across = pltpu.make_async_copy(
        w_ref.at[2, 1 - line, core, side], blocks.at[0, 2, side], loads.at[2]
    )
    near = [
        remote(blocks.at[u, 0], blocks.at[u, 1], sends.at[u], gots.at[u], other_core())
        for u in range(2)
    ]
    far = [
        remote(
            blocks.at[0, 0, 1 - side], blocks.at[0, 2, 1 - side], sends.at[2], gots.at[2], other_line()
        ),
        remote(blocks.at[1, 0], blocks.at[1, 2], sends.at[3], gots.at[3], other_line()),
    ]
    cross = [
        remote(blocks.at[u, 2], blocks.at[u, 3], sends.at[4 + u], gots.at[4 + u], other_core())
        for u in range(2)
    ]

    g_own = pltpu.make_async_copy(c_ref.at[side], g_all.at[pl.ds(0, mid)], loads.at[3])
    early = mid - mid // 4
    g_part = pltpu.make_async_copy(part_ref.at[pl.ds(0, early)], g_all.at[pl.ds(mid, early)], loads.at[4])
    g_move = remote(
        c_ref.at[1 - side, pl.ds(early, mid - early)], g_all.at[pl.ds(mid + early, mid - early)],
        sends.at[7], gots.at[7], other_side(),
    )

    @pl.when((chunk == 0) & (step == 3))
    def _():
        g_move.wait()

    @pl.when((chunk == 0) & (step == 2))
    def _():
        g_part.wait()

    @pl.when((chunk == 0) & (step == 0))
    def _():
        greet([other_core(), other_line(), other_side()])
        for copy in own:
            copy.start()
        g_move.start()
        g_own.start()
        for copy in own:
            copy.wait()
        for copy in far + near:
            copy.start()
        across.start()
        g_part.start()
        g_own.wait()

    @pl.when((chunk == 1) & (step == 0))
    def _():
        for copy in near:
            copy.wait_recv()

    @pl.when((chunk == 2) & (step == 0))
    def _():
        across.wait()
        for copy in far:
            copy.wait_recv()
        for copy in cross:
            copy.start()

    @pl.when((chunk == 3) & (step == 0))
    def _():
        for copy in cross:
            copy.wait_recv()

    y_move = remote(
        y_keep, mixed_ref.at[pl.ds(0, TILE // BLOCK)], sends.at[6], gots.at[6], other_side()
    )

    def block(which):
        return blocks[which, chunk].reshape(width, width)

    def grad_rows():
        return g_all[pl.ds(tile * per_tile, per_tile)].reshape(TILE, width)

    @pl.when(chunk == 0)
    def _():
        normal, inverse = row_stats(x_ref[rows, :].astype(F32))
        h_ref[rows, :] = (normal * vec_ref[2:3] + vec_ref[5:6]).astype(BF16)
        y_acc[rows, :] = jnp.zeros((TILE, x_ref.shape[1]), F32)
        dh_acc[rows, :] = jnp.zeros((TILE, x_ref.shape[1]), F32)

    @pl.when((chunk == 0) & (step == 0))
    def _():
        dvec_ref[...] = jnp.zeros_like(dvec_ref)

    hidden = dot(h_ref[rows, :], block(0)) + vec_ref[pl.ds(13 + hidden_block, 1)]
    grad_z = dot(grad_rows(), block(1), 1, 1)
    active, slope = gelu_pair(hidden)
    active_low = active.astype(BF16)
    grad_u = (grad_z * slope).astype(BF16)
    z_ref[rows, :] = active_low
    du_ref[rows, :] = grad_u
    y_acc[rows, :] += dot(active_low, block(1))
    dh_acc[rows, :] += dot(grad_u, block(0), 1, 1)

    @pl.when(step == steps - 1)
    def _():
        ddown_ref[0] = dot(z_ref[...], g_all[...].reshape(z_ref.shape), 0, 0).astype(BF16)
        dup_ref[0] = dot(h_ref[...], du_ref[...], 0, 0).astype(BF16)
        dvec_ref[pl.ds(3 + hidden_block, 1)] = column_sum(du_ref[...])

    @pl.when(chunk == chunks - 1)
    def _():
        start = x_ref[rows, :].astype(F32)
        result = (start + y_acc[rows, :] + vec_ref[12:13]).astype(BF16)
        y_ref[...] = result

        @pl.when(step == 0)
        def _():
            y_keep[...] = result[:TILE].reshape(y_keep.shape)
            y_move.start()

        normal, inverse = row_stats(start)
        grad_normed = dh_acc[rows, :]
        incoming = grad_rows().astype(F32)
        back = norm_pull(grad_normed, normal, inverse, vec_ref[2:3])
        dx_ref[...] = (incoming + back).astype(BF16)
        dvec_ref[0:1] += column_sum(grad_normed * normal)
        dvec_ref[1:2] += column_sum(grad_normed)
        dvec_ref[2:3] += column_sum(incoming)

    @pl.when((chunk == chunks - 1) & (step == steps - 1))
    def _():
        for copy in near + cross + far:
            copy.wait_send()
        y_move.wait()


def feed(x, cotangent, grad_part, weight_stack, vectors):
    tokens, width = x.shape
    steps = tokens // TILE
    chunks = 4
    whole = pl.BlockSpec((tokens, width), lambda j, i: (0, 0), pipeline_mode=pl.Buffered(1))
    last = pl.BlockSpec(
        (TILE, width), lambda j, i: (lax.rem(jnp.where(j == chunks - 1, i, 0) + steps // 2, steps), 0)
    )
    weight_out = pl.BlockSpec((1, width, width), lambda j, i: (j, 0, 0))
    dma = pltpu.SemaphoreType.DMA
    return pl.pallas_call(
        feed_kernel,
        grid=(chunks, steps),
        in_specs=[
            whole,
            pl.BlockSpec(vectors.shape, lambda j, i: (0, 0)),
        ]
        + [pl.BlockSpec(memory_space=pl.ANY)] * 3,
        out_specs=[
            last,
            last,
            weight_out,
            weight_out,
            pl.BlockSpec((8, width), lambda j, i: (0, 0)),
            pl.BlockSpec(memory_space=pl.ANY),
        ],
        out_shape=[
            jax.ShapeDtypeStruct((tokens, width), BF16),
            jax.ShapeDtypeStruct((tokens, width), BF16),
            jax.ShapeDtypeStruct((chunks, width, width), BF16),
            jax.ShapeDtypeStruct((chunks, width, width), BF16),
            jax.ShapeDtypeStruct((8, width), F32),
            jax.ShapeDtypeStruct((tokens // BLOCK // 2, BLOCK, width), BF16),
        ],
        scratch_shapes=[pltpu.VMEM((tokens // BLOCK, BLOCK, width), BF16)]
        + [pltpu.VMEM((tokens, width), BF16)] * 3
        + [pltpu.VMEM((tokens, width), F32)] * 2
        + [pltpu.VMEM((TILE // BLOCK, BLOCK, width), BF16)]
        + [pltpu.VMEM((2, chunks) + weight_stack.shape[3:], BF16), dma((8,)), dma((8,)), dma((6,))],
        compiler_params=pltpu.CompilerParams(
            vmem_limit_bytes=VMEM_LIMIT, collective_id=5, has_side_effects=True
        ),
        name="feed",
    )(x, vectors, weight_stack, cotangent, grad_part)


def places():
    side = lax.axis_index("seq")
    depth = lax.axis_index("clip")
    spot = lax.axis_index("fsdp")
    core = lax.rem(spot, 2)
    return side, depth, spot // 2, core


def other_core():
    _, _, line, core = places()
    return {"fsdp": 2 * line + 1 - core}


def other_side():
    return {"seq": 1 - lax.axis_index("seq")}


def other_line():
    _, _, line, core = places()
    return {"fsdp": 2 * (1 - line) + core}


def other_depth(step):
    return {"clip": lax.rem(lax.axis_index("clip") + step, lax.axis_size("clip"))}


def greet(devices):
    barrier = pltpu.get_barrier_semaphore()
    for device in devices:
        pl.semaphore_signal(barrier, inc=1, device_id=device, device_id_type=MESH)
    pl.semaphore_wait(barrier, len(devices))


def remote(source, target, send_sem, receive_sem, device):
    return pltpu.make_async_remote_copy(
        src_ref=source,
        dst_ref=target,
        send_sem=send_sem,
        recv_sem=receive_sem,
        device_id=device,
        device_id_type=MESH,
    )


def add_rows(target, source, count, rows=96):
    def one(index, carry):
        place = pl.ds(pl.multiple_of(index * rows, rows), rows)
        total = target[place, :].astype(F32) + source[place, :].astype(F32)
        target[place, :] = total.astype(target.dtype)
        return carry

    lax.fori_loop(0, count // rows, one, 0)


def attend_back_tile(
    temporal, step, x_ref, d_ref, w_ref, vec_ref, q_ref, k_ref, v_ref, p_ref, o_ref, r_ref,
    dvec_ref, dq_ref, dk_ref, dv_ref, do_ref, acc_ref, between, after=None,
):
    first = 1 if temporal else 0
    masks = half_masks()

    @pl.when(step == 0)
    def _():
        acc_ref[...] = jnp.zeros_like(acc_ref)
        dvec_ref[...] = jnp.zeros_like(dvec_ref)

    incoming = load_rows(d_ref, temporal)
    incoming_low = incoming.astype(BF16)
    do_ref[...] = (dot(incoming_low, w_ref[3], 1, 1) * r_ref[...]).astype(BF16)
    acc_ref[3] += dot(o_ref[...], incoming_low, 0, 0)
    sums = head_sums()
    scale = HEAD ** (-0.5)

    def one_block(block, carry):
        rows = pl.ds(pl.multiple_of(block * BLOCK, BLOCK), BLOCK)
        pairs = lane_pairs()
        shifted = []
        for lanes in pairs:
            grad_o = do_ref[rows, lanes]
            against = -(grad_o.astype(F32) * o_ref[rows, lanes].astype(F32))
            shifted.append(
                dot(
                    jnp.concatenate([grad_o, against.astype(BF16)], 1),
                    jnp.concatenate([stacked(v_ref[rows, lanes], masks), sums], 1),
                    1,
                    1,
                )
            )
        turned = []
        for pair in range(PAIRS):
            low = p_ref[block, pair]
            turned.append(jnp.concatenate([low[:, :BLOCK].T, low[:, BLOCK:].T], 1))
        for pair, lanes in enumerate(pairs):
            dv_ref[rows, lanes] = dot(turned[pair], stacked(do_ref[rows, lanes], masks)).astype(BF16)
        scores = [
            (p_ref[block, pair].astype(F32) * shifted[pair]).astype(BF16) for pair in range(PAIRS)
        ]
        turned = [
            jnp.concatenate([score[:, :BLOCK].T, score[:, BLOCK:].T], 1) for score in scores
        ]
        for pair, lanes in enumerate(pairs):
            dq_ref[rows, lanes] = (
                dot(scores[pair], stacked(k_ref[rows, lanes], masks)) * scale
            ).astype(BF16)
        for pair, lanes in enumerate(pairs):
            dk_ref[rows, lanes] = (
                dot(turned[pair], stacked(q_ref[rows, lanes], masks)) * scale
            ).astype(BF16)
        return carry

    lax.fori_loop(0, TILE // BLOCK, one_block, 0)
    between()
    normal, inverse = row_stats(load_rows(x_ref, temporal))
    gain_row = vec_ref[first : first + 1]
    normed = (normal * gain_row + vec_ref[first + 3 : first + 4]).astype(BF16)
    acc_ref[0] += dot(normed, dq_ref[...], 0, 0)
    acc_ref[1] += dot(normed, dk_ref[...], 0, 0)
    acc_ref[2] += dot(normed, dv_ref[...], 0, 0)
    if after is not None:
        after()
    grad_normed = (
        dot(dq_ref[...], w_ref[0], 1, 1)
        + dot(dk_ref[...], w_ref[1], 1, 1)
        + dot(dv_ref[...], w_ref[2], 1, 1)
    )
    dvec_ref[0:1] += column_sum(grad_normed * normal)
    dvec_ref[1:2] += column_sum(grad_normed)
    dvec_ref[2:3] += column_sum(dq_ref[...])
    dvec_ref[3:4] += column_sum(dv_ref[...])
    dvec_ref[4:5] += column_sum(incoming)
    return load_rows(d_ref, temporal) + norm_pull(grad_normed, normal, inverse, gain_row)


def split_sum(
    relative, source, near, local, from_x1, from_y1, from_x2, from_y2, sends, gots, loads, part=None
):
    side, depth, line, core = places()
    if relative:
        line, core = 0, 0
    rows, width = local.shape[2:]
    left = slice(0, width // 2)
    right = slice(width // 2, width)
    if part is None:
        load = pltpu.make_async_copy(source.at[:, core], local, loads)
        cores = [
            remote(
                source.at[y, 1 - core, x], near.at[y, x],
                sends.at[5 + 2 * y + x], gots.at[5 + 2 * y + x], other_core(),
            )
            for y in range(2)
            for x in range(2)
        ]
    else:
        load = pltpu.make_async_copy(source.at[:, :, part], local, loads)
        cores = []
    one_x = remote(local.at[:, 1 - side, :, left], from_x1, sends.at[1], gots.at[1], other_side())
    one_y = remote(local.at[1 - line, :, :, right], from_y1, sends.at[2], gots.at[2], other_line())
    two_y = remote(local.at[1 - line, side, :, left], from_y2, sends.at[3], gots.at[3], other_line())
    two_x = remote(local.at[line, 1 - side, :, right], from_x2, sends.at[4], gots.at[4], other_side())

    def start():
        for copy in cores:
            copy.start()
        load.start()

    def stage_one():
        load.wait()
        for copy in cores:
            copy.wait_recv()
        if cores:
            for y in range(2):
                for x in range(2):
                    add_rows(local.at[y, x], near.at[y, x], rows)
        one_x.start()
        one_y.start()

    def stage_two():
        one_x.wait_recv()
        one_y.wait_recv()
        for y in range(2):
            add_rows(local.at[y, side, :, left], from_x1.at[y], rows)
        for x in range(2):
            add_rows(local.at[line, x, :, right], from_y1.at[x], rows)
        two_y.start()
        two_x.start()

    def finish(result):
        two_y.wait_recv()
        two_x.wait_recv()
        add_rows(from_y2, local.at[line, side, :, left], rows)
        add_rows(from_x2, local.at[line, side, :, right], rows)
        result[:, left] = from_y2[...]
        result[:, right] = from_x2[...]

    def close():
        for copy in cores + [one_x, one_y, two_y, two_x]:
            copy.wait_send()

    return start, stage_one, stage_two, finish, close


def split_scratch(rows, width, near=True):
    half = width // 2
    return [
        pltpu.VMEM((2, 2, rows, width) if near else (16, width), BF16),
        pltpu.VMEM((2, 2, rows, width), BF16),
        pltpu.VMEM((2, rows, half), BF16),
        pltpu.VMEM((2, rows, half), BF16),
        pltpu.VMEM((rows, half), BF16),
        pltpu.VMEM((rows, half), BF16),
        pltpu.SemaphoreType.DMA((9,)),
        pltpu.SemaphoreType.DMA((9,)),
        pltpu.SemaphoreType.DMA,
    ]


def line_sum(relative, source, near, local, from_y, from_x, sends, gots, loads):
    side, depth, line, core = places()
    if relative:
        line, core = 0, 0
    rows = local.shape[2]
    load = pltpu.make_async_copy(source.at[:, core], local, loads)
    cores = [
        remote(
            source.at[y, 1 - core, x], near.at[y, x],
            sends.at[4 + 2 * y + x], gots.at[4 + 2 * y + x], other_core(),
        )
        for y in range(2)
        for x in range(2)
    ]
    lines = [
        remote(local.at[1 - line, x], from_y.at[x], sends.at[1 + k], gots.at[1 + k], other_line())
        for k, x in enumerate((1 - side, side))
    ]
    sides = remote(local.at[line, 1 - side], from_x, sends.at[3], gots.at[3], other_side())

    def start():
        for copy in cores:
            copy.start()
        load.start()

    def stage_one():
        load.wait()
        for copy in cores:
            copy.wait_recv()
        for y in range(2):
            for x in range(2):
                add_rows(local.at[y, x], near.at[y, x], rows)
        for copy in lines:
            copy.start()

    def stage_two():
        lines[0].wait_recv()
        add_rows(local.at[line, 1 - side], from_y.at[1 - side], rows)
        sides.start()

    def finish(result):
        lines[1].wait_recv()
        add_rows(local.at[line, side], from_y.at[side], rows)
        sides.wait_recv()
        add_rows(from_x, local.at[line, side], rows)
        result[...] = from_x[...]

    def close():
        for copy in cores + [sides] + lines:
            copy.wait_send()

    return start, stage_one, stage_two, finish, close


def line_scratch(rows, width):
    return [
        pltpu.VMEM((2, 2, rows, width), BF16),
        pltpu.VMEM((2, 2, rows, width), BF16),
        pltpu.VMEM((2, rows, width), BF16),
        pltpu.VMEM((rows, width), BF16),
        pltpu.SemaphoreType.DMA((8,)),
        pltpu.SemaphoreType.DMA((8,)),
        pltpu.SemaphoreType.DMA,
    ]


def depth_sum(owner, total, from_q, parts, q_sends, q_gots, b_sends, b_gots):
    depth = lax.axis_index("clip")
    depths = lax.axis_size("clip")
    share = total.shape[0] // depths

    def rows_of(z):
        return pl.ds(pl.multiple_of(z * share, share), share)

    def spread(step):
        to = lax.rem(depth + step, depths)
        return remote(
            total.at[rows_of(to)], from_q.at[step - 1], q_sends.at[step - 1], q_gots.at[step - 1], {"clip": to}
        )

    collect = remote(parts.at[rows_of(depth)], parts.at[rows_of(depth)], b_sends, b_gots.at[depth], {"clip": owner})

    def start():
        for step in range(1, depths):
            spread(step).start()

    def gather():
        for step in range(1, depths):
            spread(step).wait_recv()
        summed = total[rows_of(depth), :].astype(F32)
        for step in range(1, depths):
            summed = summed + from_q[step - 1].astype(F32)
        parts[rows_of(depth), :] = summed.astype(BF16)

        @pl.when(depth != owner)
        def _():
            collect.start()

    def finish():
        @pl.when(depth == owner)
        def _():
            for z in range(depths):
                if z != owner:
                    place = parts.at[rows_of(z)]
                    remote(place, place, b_sends, b_gots.at[z], other_core()).wait_recv()

    def close():
        for step in range(1, depths):
            spread(step).wait_send()

        @pl.when(depth != owner)
        def _():
            collect.wait_send()

    return start, gather, finish, close


def depth_scratch(half, width):
    depths = lax.axis_size("clip")
    dma = pltpu.SemaphoreType.DMA
    return [
        pltpu.VMEM((depths - 1, half // depths, width), BF16),
        pltpu.VMEM((half, width), BF16),
        dma((depths - 1,)),
        dma((depths - 1,)),
        dma,
        dma((depths,)),
    ]


SPLIT = 9


LINE = 7
DEPTH = 6


def back_two_kernel(
    x_ref, d_ref, w_ref, vec_ref, q_ref, k_ref, v_ref, p_ref, o_ref, r_ref, up_ref, down_ref,
    dx_ref, dw_ref, dvec_ref, up_out, down_out,
    dq_ref, dk_ref, dv_ref, do_ref, acc_ref, *sums,
):
    step = pl.program_id(0)
    side, depth, line, core = places()
    up = split_sum(True, up_ref, *sums[:SPLIT])
    down = split_sum(True, down_ref, *sums[SPLIT:])
    @pl.when(step == 0)
    def _():
        greet([other_core(), other_side(), other_line()])
        up[0]()

    @pl.when(step == 3)
    def _():
        down[2]()

    def between():
        @pl.when(step == 0)
        def _():
            up[1]()
            down[0]()

        @pl.when(step == 1)
        def _():
            down[1]()

        @pl.when(step == 2)
        def _():
            up[2]()

    result = attend_back_tile(
        True, step, x_ref, d_ref, w_ref, vec_ref, q_ref, k_ref, v_ref, p_ref, o_ref, r_ref,
        dvec_ref, dq_ref, dk_ref, dv_ref, do_ref, acc_ref, between,
    )
    store_rows(dx_ref, result, True)

    @pl.when(step == pl.num_programs(0) - 1)
    def _():
        up[3](up_out)
        down[3](down_out)
        up[4]()
        down[4]()
        dw_ref[...] = acc_ref[...].astype(BF16).reshape(dw_ref.shape)


def back_specs(full, vectors, at, rows_at, group):
    frames, patches, width = full
    rows = pl.BlockSpec((TILE, width), lambda i: (rows_at(i), 0))
    chances = pl.BlockSpec((TILE // BLOCK, PAIRS, BLOCK, 2 * BLOCK), lambda i: (rows_at(i), 0, 0, 0))
    return [
        at,
        at,
        pl.BlockSpec((4, width, width), lambda i: (group, 0, 0), pipeline_mode=pl.Buffered(1)),
        pl.BlockSpec(vectors.shape, lambda i: (0, 0)),
        rows, rows, rows, chances, rows, rows,
    ]


def back_scratch(width):
    return [pltpu.VMEM((TILE, width), BF16)] * 4 + [pltpu.VMEM((4, width, width), F32)]


def back_two(x, incoming, weight_stack, vectors, saved, d_up, d_down):
    full = x.shape
    frames, patches, width = full
    half = width // 2
    spots = TILE // frames
    at = pl.BlockSpec((frames, spots, width), lambda i: (0, i, 0))
    anywhere = pl.BlockSpec(memory_space=pl.ANY)
    vmem = pl.BlockSpec(memory_space=pltpu.VMEM)
    return pl.pallas_call(
        back_two_kernel,
        grid=(patches // spots,),
        in_specs=back_specs(full, vectors, at, lambda i: i, 1) + [anywhere] * 2,
        out_specs=[at, vmem, vmem, vmem, vmem],
        out_shape=[
            jax.ShapeDtypeStruct(full, BF16),
            jax.ShapeDtypeStruct((2, 2, 2, half, width), BF16),
            jax.ShapeDtypeStruct((8, width), F32),
            jax.ShapeDtypeStruct((half, width), BF16),
            jax.ShapeDtypeStruct((half, width), BF16),
        ],
        scratch_shapes=back_scratch(width)
        + split_scratch(half, width)
        + split_scratch(half, width),
        compiler_params=pltpu.CompilerParams(
            vmem_limit_bytes=VMEM_LIMIT, collective_id=3, has_side_effects=True
        ),
        name="back_two",
    )(
        x, incoming, weight_stack, vectors, *saved,
        d_up.reshape(2, 2, 2, half, width), d_down.reshape(2, 2, 2, half, width),
    )


def back_one_kernel(
    x_ref, d_ref, w_ref, vec_ref, q_ref, k_ref, v_ref, p_ref, o_ref, r_ref,
    two_ref, up_ref, down_ref, y_ref, mixed_in,
    one_ref, dvec_ref, two_out, early_ref, dx_out, mixed_ref, late_ref,
    dq_ref, dk_ref, dv_ref, do_ref, acc_ref, dx_all, dx_sems, late_sem, near, away, core_sems, *sums,
):
    step = pl.program_id(0)
    steps = pl.num_programs(0)
    side, depth, line, core = places()
    depths = lax.axis_size("clip")
    mid = dx_all.shape[0] // 2
    per_tile = TILE // BLOCK
    two = line_sum(False, two_ref, *sums[:LINE])
    up_parts = sums[LINE + 1]
    down_parts = sums[LINE + DEPTH + 1]
    up = depth_sum(2, up_ref, *sums[LINE : LINE + DEPTH])
    down = depth_sum(3, down_ref, *sums[LINE + DEPTH :])
    rows = one_ref.shape[2]
    cores = [
        remote(away.at[y, x], near.at[y, x], core_sems.at[0, y, x], core_sems.at[1, y, x], other_core())
        for y in range(2)
        for x in range(2)
    ]

    quarter = mid // 2
    y_move = remote(
        y_ref.at[pl.ds(mid + quarter, quarter)], mixed_ref.at[pl.ds(quarter, quarter)],
        dx_sems.at[0, 1], dx_sems.at[1, 1], other_side(),
    )
    late = pltpu.make_async_copy(dx_all.at[pl.ds(mid + per_tile, per_tile)], late_ref, late_sem)

    def dx_move(part):
        return remote(
            dx_all.at[pl.ds(mid + part * per_tile, per_tile)],
            dx_out.at[side, pl.ds(part * per_tile, per_tile)],
            dx_sems.at[0, part], dx_sems.at[1, part], other_side(),
        )

    def dx_own(part):
        return pltpu.make_async_copy(
            dx_all.at[pl.ds(part * per_tile, per_tile)],
            dx_out.at[side, pl.ds(part * per_tile, per_tile)],
            dx_sems.at[2, part],
        )

    @pl.when(step == 0)
    def _():
        greet(
            [other_core(), other_side(), other_line()]
            + [other_depth(distance) for distance in range(1, depths)]
        )
        two[0]()
        y_move.start()
        up[0]()
        down[0]()

    @pl.when(step == 1)
    def _():
        dx_move(0).start()
        two[1]()

    @pl.when(step == 2)
    def _():
        late.start()

    @pl.when(step == 3)
    def _():
        dx_own(0).start()
        down[1]()

    def between():
        @pl.when(step == 2)
        def _():
            up[1]()
            two[2]()

    def after():
        @pl.when(step == steps - 1)
        def _():
            for y in range(2):
                for x in range(2):
                    place = pl.ds(x * rows, rows)
                    away[y, x] = acc_ref[2 * y + 1 - core, place, :].astype(BF16)
                    cores[2 * y + x].start()
            for y in range(2):
                for x in range(2):
                    place = pl.ds(x * rows, rows)
                    one_ref[y, x] = acc_ref[2 * y + core, place, :].astype(BF16)

    result = attend_back_tile(
        False, step, x_ref, d_ref, w_ref, vec_ref, q_ref, k_ref, v_ref, p_ref, o_ref, r_ref,
        dvec_ref, dq_ref, dk_ref, dv_ref, do_ref, acc_ref, between, after,
    )
    tile = lax.rem(step + steps // 2, steps)
    place = pl.ds(pl.multiple_of(tile * per_tile, per_tile), per_tile)
    dx_all[place] = result.astype(BF16).reshape(per_tile, BLOCK, dx_all.shape[2])

    @pl.when(step == steps - 1)
    def _():
        dx_own(1).start()
        up[2]()
        down[2]()

        @pl.when(depth == 3)
        def _():
            early_ref[...] = down_parts[...]

        @pl.when(depth != 3)
        def _():
            early_ref[...] = up_parts[...]

        two[3](two_out)
        two[4]()
        up[3]()
        down[3]()
        for y in range(2):
            for x in range(2):
                cores[2 * y + x].wait()
                add_rows(one_ref.at[y, x], near.at[y, x], rows)
        dx_move(0).wait()
        y_move.wait()
        late.wait()
        for part in range(2):
            dx_own(part).wait()


def back_one(x, incoming, weight_stack, vectors, saved, d_two, part_up, part_down, mixed, mixed_part):
    full = x.shape
    frames, patches, width = full
    half = width // 2
    per_tile = TILE // patches
    steps = frames // per_tile
    turned = lambda i: lax.rem(i + steps // 2, steps)
    at = pl.BlockSpec((TILE, width), lambda i: (turned(i), 0))
    anywhere = pl.BlockSpec(memory_space=pl.ANY)
    vmem = pl.BlockSpec(memory_space=pltpu.VMEM)
    dma = pltpu.SemaphoreType.DMA
    return pl.pallas_call(
        back_one_kernel,
        grid=(steps,),
        in_specs=back_specs(full, vectors, at, turned, 0) + [anywhere, vmem, vmem, anywhere, anywhere],
        out_specs=[vmem] * 4 + [anywhere] * 3,
        out_shape=[
            jax.ShapeDtypeStruct((2, 2, half, width), BF16),
            jax.ShapeDtypeStruct((8, width), F32),
            jax.ShapeDtypeStruct((half, width), BF16),
            jax.ShapeDtypeStruct((half, width), BF16),
            jax.ShapeDtypeStruct((2, frames // 2, patches, width), BF16),
            jax.ShapeDtypeStruct((frames // 2, patches, width), BF16),
            jax.ShapeDtypeStruct((per_tile, patches, width), BF16),
        ],
        input_output_aliases={14: 5},
        scratch_shapes=back_scratch(width)
        + [pltpu.VMEM(full, BF16), dma((3, 2)), dma]
        + [pltpu.VMEM((2, 2, half, width), BF16)] * 2
        + [dma((2, 2, 2))]
        + line_scratch(half, width)
        + depth_scratch(half, width) * 2,
        compiler_params=pltpu.CompilerParams(
            vmem_limit_bytes=VMEM_LIMIT, collective_id=4, has_side_effects=True
        ),
        name="back_one",
    )(
        x.reshape(frames * patches, width), incoming.reshape(frames * patches, width), weight_stack, vectors,
        *saved, d_two, part_up, part_down, mixed, mixed_part,
    )


PARTS = 2


def update_kernel(
    one_ref, late_ref, two_ref, early_ref, v1_ref, v2_ref, v3_ref, vec_ref, m_ref,
    nm_ref, full, vsum_ref, vnew_ref, dx_ref,
    total, vgot, vsent, v_send, v_got, m_send, m_got, x_send, x_got, *sums,
):
    side, depth, line, core = places()
    depths = lax.axis_size("clip")
    half, width = nm_ref.shape
    share = half // PARTS
    at = SPLIT * PARTS
    one = [
        split_sum(False, one_ref, *sums[SPLIT * p : SPLIT * (p + 1)], part=p)
        for p in range(PARTS)
    ]
    one_z = [
        depth_sum(0, total.at[p], *sums[at + DEPTH * p : at + DEPTH * (p + 1)]) for p in range(PARTS)
    ]
    one_parts = [sums[at + DEPTH * p + 1] for p in range(PARTS)]
    two_z = depth_sum(1, two_ref, *sums[at + DEPTH * PARTS :])
    two_parts = sums[at + DEPTH * PARTS + 1]
    for p in range(PARTS):
        one[p][0]()
    greet(
        [other_core(), other_side(), other_line()]
        + [other_depth(step) for step in range(1, depths)]
    )
    vsent[0] = jnp.zeros(vsent.shape[1:], F32)
    order = (
        (v1_ref, 0), (v2_ref, 0), (v3_ref, 0), (v1_ref, 1), (v2_ref, 1), (v3_ref, 1),
        (v1_ref, 2), (v1_ref, 3), (v1_ref, 4), (v2_ref, 2), (v2_ref, 3), (v2_ref, 4),
        (v3_ref, 2), (v3_ref, 3), (v3_ref, 4), (v3_ref, 5), (v3_ref, 6),
    )
    for row, (ref, place) in enumerate(order):
        vsent[0, row : row + 1] = ref[place : place + 1]
    vcopies = []

    def exchange_vec(step):
        if step >= 1:
            vcopies[step - 1].wait_recv()
            if step < 3:
                vsent[step] = vsent[step - 1] + vgot[step - 1]
        if step < 3:
            device = (other_core, other_side, other_line)[step]()
            vcopies.append(remote(vsent.at[step], vgot.at[step], v_send.at[step], v_got.at[step], device))
            vcopies[-1].start()
        else:
            vgot[3 + depth] = vsent[step - 1] + vgot[step - 1]
            for distance in range(1, depths):
                vcopies.append(
                    remote(
                        vgot.at[3 + depth], vgot.at[3 + depth],
                        v_send.at[2 + distance], v_got.at[2 + distance], other_depth(distance),
                    )
                )
                vcopies[-1].start()

    def swap(p, of):
        rows = full.at[pl.ds(pl.multiple_of(of * half + p * share, 16), share)]
        return remote(rows, rows, m_send.at[p], m_got.at[p], other_side())

    def step_rows(p, grad_of):
        def one_part(index, carry):
            rows = pl.ds(pl.multiple_of(index * 48, 48), 48)
            place = pl.ds(pl.multiple_of(p * share + index * 48, 48), 48)
            moment = DECAY * m_ref[place, :] + grad_of(rows, place).astype(F32)
            nm_ref[place, :] = moment
            full[pl.ds(pl.multiple_of(side * half + p * share + index * 48, 16), 48), :] = moment.astype(BF16)
            return carry

        lax.fori_loop(0, share // 48, one_part, 0)

    def renew(p):
        @pl.when(depth == 0)
        def _():
            step_rows(p, lambda rows, place: one_parts[p][rows, :])

        @pl.when(depth == 1)
        def _():
            step_rows(p, lambda rows, place: two_parts[place, :])

        @pl.when(depth >= 2)
        def _():
            step_rows(p, lambda rows, place: early_ref[place, :])

        swap(p, side).start()

    exchange_vec(0)
    for p in range(PARTS):
        one[p][1]()
    two_z[0]()
    exchange_vec(1)
    for p in range(PARTS):
        one[p][2]()
    dx_move = remote(late_ref, dx_ref, x_send, x_got, other_side())
    dx_move.start()
    exchange_vec(2)
    two_z[1]()
    for p in range(PARTS):
        one[p][3](total.at[p])
        one_z[p][0]()
    exchange_vec(3)
    for p in range(PARTS):
        one_z[p][1]()
    two_z[2]()
    for p in range(PARTS):
        one_z[p][2]()
        renew(p)
    for distance in range(1, depths):
        remote(
            vgot.at[3], vgot.at[3 + lax.rem(depth + depths - distance, depths)],
            v_send.at[2 + distance], v_got.at[2 + distance], other_depth(distance),
        ).wait_recv()
    vsum = vgot[3]
    for z in range(1, depths):
        vsum = vsum + vgot[3 + z]
    rows = vsum_ref.shape[0]
    vsum_ref[...] = vsum[:rows]
    vnew_ref[...] = vec_ref[...] - VECTOR_RATE * (65536.0 ** (-0.5)) * vsum[:rows]
    for p in range(PARTS):
        swap(p, 1 - side).wait_recv()
        one[p][4]()
        one_z[p][3]()
    two_z[3]()
    dx_move.wait()
    for copy in vcopies:
        copy.wait_send()
    for p in range(PARTS):
        swap(p, side).wait_send()


def update(d_one, late, part_two, early, vec_one, vec_two, vec_three, vectors, momentum):
    half, width = momentum.shape
    depths = lax.axis_size("clip")
    dma = pltpu.SemaphoreType.DMA
    anywhere = pl.BlockSpec(memory_space=pl.ANY)
    vmem = pl.BlockSpec(memory_space=pltpu.VMEM)
    return pl.pallas_call(
        update_kernel,
        in_specs=[anywhere] * 2 + [vmem] * 7,
        out_specs=[vmem] * 4 + [anywhere],
        out_shape=[
            jax.ShapeDtypeStruct((half, width), F32),
            jax.ShapeDtypeStruct((width, width), BF16),
            jax.ShapeDtypeStruct(vectors.shape, F32),
            jax.ShapeDtypeStruct(vectors.shape, F32),
            jax.ShapeDtypeStruct(late.shape, BF16),
        ],
        scratch_shapes=[
            pltpu.VMEM((PARTS, half // PARTS, width), BF16),
            pltpu.VMEM((3 + depths, 24, width), F32),
            pltpu.VMEM((3, 24, width), F32),
            dma((2 + depths,)), dma((2 + depths,)),
            dma((PARTS,)), dma((PARTS,)),
            dma, dma,
        ]
        + split_scratch(half // PARTS, width, False) * PARTS
        + depth_scratch(half // PARTS, width) * PARTS
        + depth_scratch(half, width),
        compiler_params=pltpu.CompilerParams(
            vmem_limit_bytes=VMEM_LIMIT, collective_id=1, has_side_effects=True
        ),
        name="update",
    )(d_one.reshape(2, 2, PARTS, half // PARTS, width), late, part_two, early, vec_one, vec_two, vec_three, vectors, momentum)


def finish_kernel(
    full, w_ref, nm_in, vsum_in, vnew_in, y_in, mixed_in, dx_in, late_in,
    nw_ref, low_ref, nm_ref, vsum_ref, vnew_ref, mixed_ref, dx_ref,
    x_acc, a_low, p_low, y_all, dx_all, sems,
):
    side, depth, line, core = places()
    half = w_ref.shape[0]
    mid = mixed_in.shape[0]
    loads = [
        pltpu.make_async_copy(y_in.at[pl.ds(0, mid)], y_all.at[side], sems.at[0]),
        pltpu.make_async_copy(mixed_in, y_all.at[1 - side], sems.at[1]),
        pltpu.make_async_copy(dx_in.at[side], dx_all.at[side], sems.at[2]),
        pltpu.make_async_copy(
            dx_in.at[1 - side, pl.ds(0, mid // 2)], dx_all.at[1 - side, pl.ds(0, mid // 2)], sems.at[5]
        ),
        pltpu.make_async_copy(late_in, dx_all.at[1 - side, pl.ds(mid // 2, mid // 2)], sems.at[6]),
    ]
    stores = [
        pltpu.make_async_copy(y_all, mixed_ref, sems.at[3]),
        pltpu.make_async_copy(dx_all, dx_ref, sems.at[4]),
    ]
    for copy in loads:
        copy.start()
    nm_ref[...] = nm_in[...]
    vsum_ref[...] = vsum_in[...]
    vnew_ref[...] = vnew_in[...]
    mine = pl.ds(pl.multiple_of(side * half, half), half)
    moment = full[...].astype(F32)
    squares = jnp.sum(jnp.sum(moment * moment, 0, keepdims=True), 1, keepdims=True)
    x_acc[...] = moment * (1.0 / (jnp.sqrt(squares) + 1e-07))
    for sweep in range(NS_STEPS):
        low = x_acc[...].astype(BF16)
        gram = dot(low, low, 1, 1)
        a_low[...] = gram.astype(BF16)
        if sweep < NS_STEPS - 1:
            p_low[...] = (NS_B * gram + NS_C * dot(a_low[...], a_low[...])).astype(BF16)
            x_acc[...] = NS_A * x_acc[...] + dot(p_low[...], low)
            for copy in loads:
                copy.wait()
            for copy in stores:
                copy.start()
        else:
            part = a_low[mine, :]
            power = (NS_B * part.astype(F32) + NS_C * dot(part, a_low[...])).astype(BF16)
            block = 4 * depth + 2 * line + core
            factor = jnp.where(block == 3, 4.0, jnp.where(block == 7, 2.0, jnp.where(block >= 12, 0.5, 1.0)))
            result = NS_A * x_acc[mine, :] + dot(power, low)
            renewed = w_ref[...] - MUON_RATE * factor * result
            nw_ref[...] = renewed
            low_ref[...] = renewed.astype(BF16)
    for copy in stores:
        copy.wait()


def finish(full, weights, new_momentum, vector_sum, new_vectors, y, mixed, dx, late):
    half, width = weights.shape
    anywhere = pl.BlockSpec(memory_space=pl.ANY)
    vmem = pl.BlockSpec(memory_space=pltpu.VMEM)
    return pl.pallas_call(
        finish_kernel,
        in_specs=[vmem] * 5 + [anywhere] * 4,
        out_specs=[vmem] * 5 + [anywhere] * 2,
        out_shape=[
            jax.ShapeDtypeStruct((half, width), F32),
            jax.ShapeDtypeStruct((half, width), BF16),
            jax.ShapeDtypeStruct((half, width), F32),
            jax.ShapeDtypeStruct(vector_sum.shape, F32),
            jax.ShapeDtypeStruct(vector_sum.shape, F32),
            jax.ShapeDtypeStruct(dx.shape, BF16),
            jax.ShapeDtypeStruct(dx.shape, BF16),
        ],
        scratch_shapes=[
            pltpu.VMEM((width, width), F32),
            pltpu.VMEM((width, width), BF16),
            pltpu.VMEM((width, width), BF16),
            pltpu.VMEM(dx.shape, BF16),
            pltpu.VMEM(dx.shape, BF16),
            pltpu.SemaphoreType.DMA((7,)),
        ],
        compiler_params=pltpu.CompilerParams(vmem_limit_bytes=VMEM_LIMIT),
        name="finish",
    )(full, weights, new_momentum, vector_sum, new_vectors, y, mixed, dx, late)


def attend_tile(temporal, start, weight, vec_ref, q_ref, k_ref, v_ref, p_ref, o_ref, r_ref):
    first = 1 if temporal else 0
    bias = 9 if temporal else 6
    normal, inverse = row_stats(start)
    normed = (normal * vec_ref[first : first + 1] + vec_ref[first + 3 : first + 4]).astype(BF16)
    q_ref[...] = (dot(normed, weight(0)) + vec_ref[bias : bias + 1]).astype(BF16)
    k_ref[...] = dot(normed, weight(1)).astype(BF16)
    v_ref[...] = (dot(normed, weight(2)) + vec_ref[bias + 1 : bias + 2]).astype(BF16)
    masks = half_masks()
    mask = place_mask() if temporal else None
    sums = head_sums()

    def one_block(block, carry):
        rows = pl.ds(pl.multiple_of(block * BLOCK, BLOCK), BLOCK)
        pairs = lane_pairs()
        scores = [dot(q_ref[rows, lanes], stacked(k_ref[rows, lanes], masks), 1, 1) for lanes in pairs]
        powers = [powers_of(score, mask) for score in scores]
        mixes = []
        for pair, lanes in enumerate(pairs):
            p_ref[block, pair] = powers[pair]
            values = jnp.concatenate([stacked(v_ref[rows, lanes], masks), sums], 1)
            mixes.append(dot(powers[pair], values))
        for mix, lanes in zip(mixes, pairs):
            inverse_sum = 1.0 / mix[:, BLOCK:]
            r_ref[rows, lanes] = inverse_sum
            o_ref[rows, lanes] = (mix[:, :BLOCK] * inverse_sum).astype(BF16)
        return carry

    lax.fori_loop(0, TILE // BLOCK, one_block, 0)
    return dot(o_ref[...], weight(3)) + vec_ref[bias + 2 : bias + 3]


PIECES = 4
ARRIVALS = {
    (2, 2): (1, 1),
    (2, 3): (0, 1),
    (1, 2): (0, 2),
    (1, 3): (2, 3),
    (3, 2): (5, 8),
    (0, 2): (5, 8),
    (0, 3): (8, 8),
}
SECOND = {0: (0, 2), 2: (-1, 0), 3: (1, 2)}


def front_kernel(
    t_ref, g_ref, w_ref, vec_ref,
    w_out, x_out, g_out,
    q1_ref, k1_ref, v1_ref, p1_ref, o1_ref, r1_ref, y1_ref,
    q2_ref, k2_ref, v2_ref, p2_ref, o2_ref, r2_ref, y2_ref,
    w_all, x_all, x1_all,
    near_send, near_got, up_send, up_got, sx_send, sx_got, sy_send, sy_got, di_send, di_got,
    px_send, px_got, pz_send, pz_got, py_send, py_got, pc_send, pc_got,
    su_send, su_got, sl_send, sl_got,
    tok_send, tok_got, load_sem,
):
    step = pl.program_id(0)
    side, depth, line, core = places()
    depths = lax.axis_size("clip")
    last = depths - 1
    half, width = w_ref.shape
    frames = x_all.shape[0]
    mid = frames // 2
    per_tile = TILE // x_all.shape[1]
    halves = pl.num_programs(0) // 2
    left = slice(0, width // 2)
    right = slice(width // 2, width)

    def piece(g, h):
        return w_all.at[g, line, core, side if h == 0 else 1 - side]

    def move_up(g, h):
        return remote(piece(g, h), piece(g, h), pz_send.at[g, h, 0], pz_got.at[g, h], {"clip": depth + 1})

    def move_down(g, h):
        return remote(piece(g, h), piece(g, h), pz_send.at[g, h, 1], pz_got.at[g, h], {"clip": depth - 1})

    def move_line(g, h):
        return remote(piece(g, h), piece(g, h), py_send.at[g, h], py_got.at[g, h], other_line())

    def from_line(g, h):
        place = w_all.at[g, 1 - line, core, side if h == 0 else 1 - side]
        return remote(place, place, py_send.at[g, h], py_got.at[g, h], other_line())

    core_parts = [(line, None), (1 - line, 0), (1 - line, 1)]

    def second_core(part, received=False):
        line_at, h = core_parts[part]
        place = w_all.at[1, line_at, 1 - core if received else core]
        if h is not None:
            place = place.at[side if h == 0 else 1 - side]
        return remote(place, place, pc_send.at[part], pc_got.at[part], other_core())

    own_side = remote(piece(depth, 0), piece(depth, 0), px_send, px_got, other_side())
    from_side = remote(piece(depth, 1), piece(depth, 1), px_send, px_got, other_side())

    def token_move(part):
        return remote(
            x1_all.at[pl.ds(mid + part * per_tile, per_tile)],
            x_all.at[pl.ds(mid + part * per_tile, per_tile)],
            tok_send.at[part], tok_got.at[part], other_side(),
        )

    token_parts = mid // per_tile

    def grad_move(part):
        place = (pl.ds(0, mid // 2), pl.ds(mid // 2, mid // 4))[part]
        return remote(
            g_ref.at[1 - side, place], g_out.at[place],
            tok_send.at[token_parts + part], tok_got.at[token_parts + part], other_side(),
        )

    token_own = pltpu.make_async_copy(t_ref.at[side], x_all.at[pl.ds(0, mid)], load_sem.at[0])
    token_other = pltpu.make_async_copy(t_ref.at[1 - side], x1_all.at[pl.ds(mid, mid)], load_sem.at[7])
    outs = [
        pltpu.make_async_copy(place, target, load_sem.at[1 + k])
        for k, (place, target) in enumerate(
            [(w_all.at[g], w_out.at[g]) for g in range(2)]
            + [(w_all.at[g, line, core], w_out.at[g, line, core]) for g in range(2, depths)]
            + [(w_all.at[2, 1 - line, core, side], w_out.at[2, 1 - line, core, side])]
        )
    ]
    keep = pltpu.make_async_copy(x_all, x_out, load_sem.at[6])

    def arrive(g, h, at):
        @pl.when(depth == at)
        def _():
            if at != g:
                move_up(g, h).wait_recv()
            if g <= at < last:
                move_up(g, h).start()
            if 0 < at < g:
                move_down(g, h).start()
            if (g, h) == (2, 0):
                move_line(g, h).start()

    def second(e, line_at):
        rows = pl.ds((e % 2) * (half // 2), half // 2)
        return w_all.at[1, line_at, core, side if e < 2 else 1 - side, rows]

    def second_up(e):
        return same(second(e, line), su_send.at[e], su_got.at[e], {"clip": depth + 1})

    def second_line(e, received=False):
        return same(second(e, 1 - line if received else line), sl_send.at[e], sl_got.at[e], other_line())

    def arrivals(slot):
        for at, slots in SECOND.items():
            for h in range(2):
                if slots[h] == slot:

                    @pl.when(depth == at)
                    def _():
                        if at == 0:
                            move_up(1, h).wait_recv()
                        for e in (2 * h, 2 * h + 1):
                            if at > 0:
                                second_up(e).wait_recv()
                            if 0 < at < last:
                                second_up(e).start()
                            second_line(e).start()

        for (at, g), slots in ARRIVALS.items():
            for h in range(2):
                if slots[h] == slot:
                    arrive(g, h, at)

    def first(k, line_at, side_at, columns=slice(None)):
        return w_all.at[0, line_at, core, side_at, pl.ds(k * (half // PIECES), half // PIECES), columns]

    def same(place, send, got, device):
        return remote(place, place, send, got, device)

    def first_up(k):
        return same(first(k, line, side), up_send.at[k], up_got.at[k], {"clip": depth + 1})

    def first_side(k, received=False):
        return same(first(k, line, 1 - side if received else side), sx_send.at[k], sx_got.at[k], other_side())

    def first_line(k, received=False):
        return same(first(k, 1 - line if received else line, side), sy_send.at[k], sy_got.at[k], other_line())

    def first_cross(k, way, received=False):
        if received:
            place = first(k, 1 - line, 1 - side, (left, right)[way])
        elif way == 0:
            place = first(k, 1 - line, side, left)
        else:
            place = first(k, line, 1 - side, right)
        return same(place, di_send.at[k, way], di_got.at[k, way], (other_side, other_line)[way]())

    spots = [(line, side), (1 - line, side), (line, 1 - side), (1 - line, 1 - side)]

    def first_core(k, spot, received=False):
        line_at, side_at = spots[spot]
        place = w_all.at[
            0, line_at, 1 - core if received else core, side_at, pl.ds(k * (half // PIECES), half // PIECES)
        ]
        return same(place, near_send.at[k, spot], near_got.at[k, spot], other_core())

    @pl.when(step == 0)
    def _():
        greet(
            [other_core(), other_side(), other_line()]
            + [other_depth(distance) for distance in range(1, depths)]
        )
        token_own.start()
        token_other.start()
        w_all[depth, line, core, side] = w_ref[...].astype(BF16)

        @pl.when(depth > 0)
        def _():
            own_side.start()

        @pl.when(depth > 0)
        def _():
            move_down(depth, 0).start()

        for k in range(PIECES):

            @pl.when(depth > 0)
            def _():
                first_up(k).wait_recv()

            @pl.when(depth < last)
            def _():
                first_up(k).start()

            first_side(k).start()
            first_line(k).start()
            first_core(k, 0).start()

        @pl.when(depth == 1)
        def _():
            for e in (0, 1):
                second_up(e).start()

        @pl.when(depth > 0)
        def _():
            from_side.wait_recv()
            move_down(depth, 1).start()

        @pl.when(depth == 1)
        def _():
            for e in (2, 3):
                second_up(e).start()
            for e in range(4):
                second_line(e).start()

        for k in range(PIECES):
            first_line(k, True).wait_recv()
            first_cross(k, 0).start()
            first_core(k, 1).start()
            first_side(k, True).wait_recv()
            first_cross(k, 1).start()
            first_core(k, 2).start()
        arrivals(-1)
        token_other.wait()
        token_move(0).start()
        for k in range(PIECES):
            first_cross(k, 0, True).wait_recv()
            first_cross(k, 1, True).wait_recv()
            first_core(k, 3).start()
        for k in range(PIECES):
            for spot in range(4):
                first_core(k, spot, True).wait_recv()
        token_move(1).start()
        arrivals(0)
        token_own.wait()

    for slot in range(1, 8):

        @pl.when(step == slot)
        def _():
            if slot == 1:
                outs[0].start()
            if slot == 2:
                token_move(0).wait()
            if slot == 3:
                token_move(1).wait()
                grad_move(0).start()
                keep.start()
            arrivals(slot)
            if slot == 2:
                second_core(0).start()
            if slot == 3:
                for e in range(2):
                    second_line(e, True).wait_recv()
                second_core(1).start()
            if slot == 5:
                grad_move(1).start()
            if slot == 4:
                for e in range(2, 4):
                    second_line(e, True).wait_recv()
                second_core(2).start()
                for part in range(3):
                    second_core(part, True).wait_recv()
                outs[1].start()

    @pl.when(step < halves)
    def _():
        place = pl.ds(pl.multiple_of(step * per_tile, per_tile), per_tile)
        start = x_all[place].astype(F32).reshape(TILE, width)
        branch = attend_tile(
            False, start, lambda b: w_all[0, b // 2, b % 2].reshape(width, width), vec_ref,
            q1_ref, k1_ref, v1_ref, p1_ref, o1_ref, r1_ref,
        )
        start = x_all[place].astype(F32).reshape(TILE, width)
        result = (start + branch).astype(BF16).reshape(per_tile, BLOCK, width)
        y1_ref[...] = result
        x1_all[place] = result

    @pl.when(step >= halves)
    def _():
        spots = TILE // frames
        place = pl.ds(pl.multiple_of((step - halves) * spots, spots), spots)
        tile_ref = x1_all.at[:, place, :]
        branch = attend_tile(
            True, load_rows(tile_ref, True), lambda b: w_all[1, b // 2, b % 2].reshape(width, width), vec_ref,
            q2_ref, k2_ref, v2_ref, p2_ref, o2_ref, r2_ref,
        )
        store_rows(y2_ref, load_rows(tile_ref, True) + branch, True)

    @pl.when(step == 2 * halves - 1)
    def _():
        arrivals(8)
        from_line(2, 0).wait_recv()
        for copy in outs[2:]:
            copy.start()
        for part in range(2):
            grad_move(part).wait()
        keep.wait()
        for copy in outs:
            copy.wait()

        @pl.when(depth > 0)
        def _():
            own_side.wait_send()

        for k in range(PIECES):

            @pl.when(depth < last)
            def _():
                first_up(k).wait_send()

            first_side(k).wait_send()
            first_line(k).wait_send()
            first_cross(k, 0).wait_send()
            first_cross(k, 1).wait_send()
            for spot in range(4):
                first_core(k, spot).wait_send()
        for h in range(2):

            @pl.when(depth == 2)
            def _():
                move_up(2, h).wait_send()

            for g in range(1, depths):

                @pl.when((depth > 0) & (depth <= g))
                def _():
                    move_down(g, h).wait_send()

        for e in range(4):

            @pl.when((depth > 0) & (depth < last))
            def _():
                second_up(e).wait_send()

            second_line(e).wait_send()
        move_line(2, 0).wait_send()
        for part in range(3):
            second_core(part).wait_send()


def front(tokens, cotangent, weights, vectors):
    _, mid, patches, width = tokens.shape
    half = weights.shape[0]
    frames = 2 * mid
    count = frames * patches
    halves = count // TILE
    depths = lax.axis_size("clip")
    dma = pltpu.SemaphoreType.DMA
    anywhere = pl.BlockSpec(memory_space=pl.ANY)
    one = lambda i: jnp.minimum(i, halves - 1)
    two = lambda i: jnp.maximum(i - halves, 0)

    def saved(at):
        rows = pl.BlockSpec((TILE, width), lambda i: (at(i), 0))
        chances = pl.BlockSpec((TILE // BLOCK, PAIRS, BLOCK, 2 * BLOCK), lambda i: (at(i), 0, 0, 0))
        return [rows, rows, rows, chances, rows, rows]

    rows_shape = jax.ShapeDtypeStruct((count, width), BF16)
    saved_shape = [
        rows_shape,
        rows_shape,
        rows_shape,
        jax.ShapeDtypeStruct((count // BLOCK, PAIRS, BLOCK, 2 * BLOCK), BF16),
        rows_shape,
        jax.ShapeDtypeStruct((count, width), F32),
    ]
    full = jax.ShapeDtypeStruct((frames, patches, width), BF16)
    stack = (depths, 2, 2, 2, half, width)
    outs = pl.pallas_call(
        front_kernel,
        grid=(2 * halves,),
        in_specs=[
            anywhere,
            anywhere,
            pl.BlockSpec((half, width), lambda i: (0, 0), pipeline_mode=pl.Buffered(1)),
            pl.BlockSpec(vectors.shape, lambda i: (0, 0)),
        ],
        out_specs=[anywhere] * 3
        + saved(one)
        + [pl.BlockSpec((TILE // patches, patches, width), lambda i: (one(i), 0, 0))]
        + saved(two)
        + [pl.BlockSpec((frames, TILE // frames, width), lambda i: (0, two(i), 0))],
        out_shape=[
            jax.ShapeDtypeStruct(stack, BF16),
            full,
            jax.ShapeDtypeStruct((mid, patches, width), BF16),
        ]
        + saved_shape
        + [full]
        + saved_shape
        + [full],
        scratch_shapes=[
            pltpu.VMEM(stack, BF16),
            pltpu.VMEM((frames, patches, width), BF16),
            pltpu.VMEM((frames, patches, width), BF16),
            dma((PIECES, 4)), dma((PIECES, 4)),
            dma((PIECES,)), dma((PIECES,)),
            dma((PIECES,)), dma((PIECES,)),
            dma((PIECES,)), dma((PIECES,)),
            dma((PIECES, 2)), dma((PIECES, 2)),
            dma, dma,
            dma((depths, 2, depths)), dma((depths, 2)),
            dma((depths, 2)), dma((depths, 2)),
            dma((depths,)), dma((depths,)),
            dma((4,)), dma((4,)),
            dma((4,)), dma((4,)),
            dma((mid * patches // TILE + 2,)), dma((mid * patches // TILE + 2,)),
            dma((8,)),
        ],
        compiler_params=pltpu.CompilerParams(
            vmem_limit_bytes=VMEM_LIMIT, collective_id=2, has_side_effects=True
        ),
        name="front",
    )(tokens, cotangent, weights, vectors)
    stacked_weights, x0, gy = outs[:3]
    return stacked_weights, x0, gy, outs[3:9], outs[9], outs[10:16], outs[16]


def paired_body(tokens, cotangent, weights, momentum, vectors):
    weight_stack, x0, grad_part, saved_one, x1, saved_two, x2 = front(
        tokens[:, 0], cotangent[:, 0], weights[0], vectors
    )
    full = x0.shape
    mixed, dx2, d_up, d_down, vec_three, mixed_part = feed(
        x2.reshape(full[0] * full[1], full[2]), cotangent[:, 0], grad_part, weight_stack, vectors
    )
    mixed = mixed.reshape(full)
    weight_stack = weight_stack.reshape(-1, full[2], full[2])
    dx1, d_two, vec_two, part_up, part_down = back_two(
        x1, dx2.reshape(full), weight_stack, vectors, saved_two, d_up, d_down
    )
    d_one, vec_one, part_two, early, grad_out, mixed_part, late = back_one(
        x0, dx1, weight_stack, vectors, saved_one, d_two, part_up, part_down, mixed, mixed_part
    )
    new_momentum, moment, vector_sum, new_vectors, late = update(
        d_one, late, part_two, early, vec_one, vec_two, vec_three, vectors, momentum[0]
    )
    new_weights, new_low, new_momentum, vector_sum, new_vectors, mixed_out, grad_out = finish(
        moment, weights[0], new_momentum, vector_sum, new_vectors, mixed, mixed_part, grad_out, late
    )
    return (
        mixed_out[:, None],
        grad_out[:, None],
        new_momentum[None],
        new_weights[None],
        new_low[None],
        vector_sum,
        new_vectors,
    )


def solution(mesh):
    in_specs = (
        P(None, ("clip", "fsdp"), "seq", None, None),
        P(None, ("clip", "fsdp"), "seq", None, None),
        P(("clip", "fsdp"), "seq", None),
        P(("clip", "fsdp"), "seq", None),
        P(),
    )
    out_specs = (
        P(None, ("clip", "fsdp"), "seq", None, None),
        P(None, ("clip", "fsdp"), "seq", None, None),
        P(("clip", "fsdp"), "seq", None),
        P(("clip", "fsdp"), "seq", None),
        P(("clip", "fsdp"), "seq", None),
        P(),
        P(),
    )
    paired = dict(mesh.shape) == {"clip": 4, "seq": 2, "fsdp": 4}
    program = paired_body if paired else body
    return jax.shard_map(program, mesh=mesh, in_specs=in_specs, out_specs=out_specs, check_vma=False)
```
